32 devices in a mesh: table: 4 (over x, core), tensor: 2 (over y), dp: 4 (over z).
Axes of the slice: x: 2, y: 2, z: 4, core: 2. Of those that a mesh axis runs over, the one named last changes fastest.
Arguments:
- lookup_ids: int32 [2048, 4, 16], P('dp', 'table'), may hold values from 0 to 4095
- bag_lengths: int32 [2048, 4], P('dp', 'table'), may hold values from 1 to 16
- feature_widths: int32 [4], replicated, may hold values from 32 to 256, as said below
- tables: bfloat16 [4, 4096, 256], P('table', None, 'tensor'), may hold values from -6 to 6
- w_in: bfloat16 [1024, 16384], P(None, ('table', 'tensor')), may hold values from -0.5 to 0.5
- w_out: bfloat16 [16384, 4096], P(('table', 'tensor')), may hold values from -0.125 to 0.125
- cotangent: bfloat16 [2048, 4096], P('dp', ('table', 'tensor')), may hold values from -6 to 6
Outputs:
- mixed_out: bfloat16 [2048, 4096], P('dp', ('table', 'tensor'))
- grad_in: float32 [1024, 16384], P('dp', ('table', 'tensor'))
- grad_out: float32 [16384, 4096], P(('table', 'tensor', 'dp'))
The draws below stay inside these ranges and needn't reach their ends.
Inputs may be any that keep to these rules, and one draw needn't show every extreme that they name: `feature_widths`: multiples of 32; one feature has exactly 256, another exactly 32.
All inputs are finite; a program needn't handle non-finite values.
Results may differ from the reference program's by a relative error of at most 0.0056.
Values may be sent and summed in bfloat16 or wider, within the bound.
No kernel may reach another device: no remote copies, remote signals or barrier semaphores. Data moves between devices by JAX's collectives and lax.ppermute only.
A program may use at most 128 MiB of HBM per device.

```python
import jax
import jax.numpy as jnp
from jax import lax

EMB = 256
H = 16384
OUT = 4096
VOCAB = 4096
BAG = 16
FEATS = 4
IN = 1024
SAMPLES = 2048


def draw_feature_widths(key, part):
    key_levels = jax.random.fold_in(key, 11)
    key_pick = jax.random.fold_in(key, 23)
    levels = jax.random.randint(key_levels, (FEATS,), 1, 9)
    chosen = jax.random.randint(key_pick, (), 0, FEATS)
    positions = jnp.arange(FEATS)
    levels = jnp.where(positions == chosen, 8, jnp.where(positions == (chosen + 1) % FEATS, 1, levels))
    return (levels * (EMB // 8)).astype(jnp.int32)


def place_ends(result, own_key, low, largest):
    extent = result.shape
    index_at = [jax.random.randint(jax.random.fold_in(own_key, axis), (), 0, extent[axis]) for axis in range(len(extent))]
    result = result.at[tuple(index_at)].set(low)
    longest = extent.index(max(extent))
    index_at[longest] = (index_at[longest] + 1) % extent[longest]
    return result.at[tuple(index_at)].set(largest)


def raised(drawn, rng, source, target, shards_of, factor):
    def block_of(dim):
        return (jnp.arange(drawn.shape[dim]) // (drawn.shape[dim] // shards_of)).reshape((-1,) + (1,) * (drawn.ndim - 1 - dim))

    near = jax.random.permutation(rng, shards_of)[block_of(target)]
    second = (block_of(target) + shards_of // 2) % shards_of
    return jnp.where((block_of(source) == near) | (block_of(source) == second), factor * drawn, drawn)


def level_of(key, shape, shards, least, top_value):
    factor_of = 1.0
    for position, blocks in shards:
        draws = jax.random.uniform(jax.random.fold_in(jax.random.fold_in(key, 6), position), (blocks,), jnp.float32, least / len(shards), top_value / len(shards))
        factor_of = factor_of * jnp.repeat(jnp.exp(draws), shape[position] // blocks).reshape((-1,) + (1,) * (len(shape) - 1 - position))
    return factor_of


def scatter_about(stream_key, extent, scale, bound, cuts=(), held_as=jnp.bfloat16):
    entries = scale * jax.random.normal(stream_key, extent, jnp.float32)
    if cuts:
        entries = entries * level_of(stream_key, extent, cuts, -0.22, 0.18)
    return jnp.clip(entries, -bound, bound).astype(held_as)


def noise_with(stream_key, extent, scale, limit, split, heavy, held_as=jnp.bfloat16):
    entries = scale * jax.random.normal(stream_key, extent, jnp.float32)
    if split:
        entries = entries * level_of(stream_key, extent, split, -0.22, 0.18)
    return jnp.clip(raised(entries, jax.random.fold_in(stream_key, 3), *heavy), -limit, limit).astype(held_as)


def setup_inputs(seed: int = 0) -> dict:
    key_of = jax.random.split(jax.random.key(seed), 8)
    lookup_ids = place_ends(jax.random.randint(key_of[0], (SAMPLES, FEATS, BAG), 0, VOCAB), jax.random.fold_in(key_of[0], 1), 0, VOCAB - 1).astype(jnp.int32)
    bag_lengths = place_ends(jax.random.randint(key_of[1], (SAMPLES, FEATS), 1, BAG + 1), jax.random.fold_in(key_of[1], 1), 1, BAG).astype(jnp.int32)
    feature_widths = draw_feature_widths(jax.random.fold_in(key_of[7], 71), 0)
    tables = scatter_about(key_of[3], (FEATS, VOCAB, EMB), 1.0, 6.0, ((0, 4), (2, 2)))
    w_in = scatter_about(key_of[4], (IN, H), (IN // 8) ** -0.5, 0.5, ((1, 8),))
    w_out = noise_with(key_of[5], (H, OUT), (H // 4) ** -0.5, 0.125, ((0, 8),), (0, 1, 8, 2.0))
    cotangent = scatter_about(key_of[6], (SAMPLES, OUT), 1.0, 6.0, ((0, 4), (1, 8)))
    return {"lookup_ids": lookup_ids, "bag_lengths": bag_lengths, "feature_widths": feature_widths, "tables": tables, "w_in": w_in, "w_out": w_out, "cotangent": cotangent}


def silu_slope(preact):
    sigmoid_part = jax.nn.sigmoid(preact)
    return sigmoid_part * (1.0 + preact * (1.0 - sigmoid_part))


def pool_feature(inputs):
    lookup, lengths, embedding, width = inputs
    in_bag = jnp.arange(BAG)[None, :] < lengths[:, None]
    vocab_ids = jnp.arange(VOCAB).astype(jnp.int32)
    counts = jnp.zeros((lookup.shape[0], VOCAB), jnp.float32)
    for slot_index in range(BAG):
        hits = (lookup[:, slot_index:slot_index + 1] == vocab_ids[None, :]) & in_bag[:, slot_index:slot_index + 1]
        counts = counts + hits.astype(jnp.float32)
    summed = jnp.dot(counts.astype(jnp.bfloat16), embedding, preferred_element_type=jnp.float32)
    pooled = summed / lengths[:, None].astype(jnp.float32)
    keep = jnp.arange(EMB)[None, :] < width
    return jnp.where(keep, pooled, jnp.zeros_like(pooled)).astype(jnp.bfloat16)


def reference(lookup_ids, bag_lengths, feature_widths, tables, w_in, w_out, cotangent):
    pooled = lax.map(pool_feature, (jnp.transpose(lookup_ids, (1, 0, 2)), jnp.transpose(bag_lengths), tables, feature_widths))
    features = jnp.transpose(pooled, (1, 0, 2)).reshape(SAMPLES, IN)
    preact = jnp.dot(features, w_in, preferred_element_type=jnp.float32)
    hidden = jax.nn.silu(preact).astype(jnp.bfloat16)
    mixed_out = jnp.dot(hidden, w_out, preferred_element_type=jnp.float32).astype(jnp.bfloat16)
    grad_hidden = jnp.dot(cotangent, w_out.T, preferred_element_type=jnp.float32)
    grad_preact = (grad_hidden * silu_slope(preact)).astype(jnp.bfloat16)
    grad_in = jnp.dot(features.T, grad_preact, preferred_element_type=jnp.float32)
    grad_out = jnp.dot(hidden.T, cotangent, preferred_element_type=jnp.float32)
    return (mixed_out, grad_in, grad_out)
```

```python
import functools

import jax
import jax.numpy as jnp
from jax import lax
from jax.experimental import pallas as pl
from jax.experimental.pallas import tpu as pltpu
from jax.sharding import PartitionSpec as P

F32 = jnp.float32
BF16 = jnp.bfloat16
PLANE = ("table", "tensor")
ROWS_TN = (((0,), (0,)), ((), ()))
COLS_NT = (((1,), (1,)), ((), ()))


def silu_slope(preact):
    sigmoid_part = jax.nn.sigmoid(preact)
    return sigmoid_part * (1.0 + preact * (1.0 - sigmoid_part))


def params(mib):
    return pltpu.CompilerParams(vmem_limit_bytes=mib * 1024 * 1024)


def pool_kernel(width_ref, hi_ref, lo_ref, len_ref, table_ref, out_ref, counts_ref, *, group, low):
    samples = out_ref.shape[0]
    slots = hi_ref.shape[1]
    high = table_ref.shape[0] // low
    rows = lax.broadcasted_iota(jnp.int32, (high * group, slots), 0)
    low_rows = lax.broadcasted_iota(jnp.int32, (low, slots), 0)

    def one_group(g, carry):
        hit_high = (rows == hi_ref[pl.ds(g, 1), :]).astype(BF16)
        hit_low = (low_rows == lo_ref[pl.ds(g, 1), :]).astype(BF16)
        counts = lax.dot_general(hit_high, hit_low, COLS_NT, preferred_element_type=F32).astype(BF16)
        first = pl.multiple_of(g * group, group)
        for h in range(high):
            counts_ref[h, pl.ds(first, group), :] = counts[h * group : (h + 1) * group, :]
        return carry

    lax.fori_loop(0, samples // group, one_group, 0)
    total = jnp.zeros(out_ref.shape, F32)
    for h in range(high):
        total += jnp.dot(
            counts_ref[h], table_ref[h * low : (h + 1) * low, :], preferred_element_type=F32
        )
    pooled = total / len_ref[...].astype(F32)
    columns = width_ref[1] + lax.broadcasted_iota(jnp.int32, pooled.shape, 1)
    out_ref[...] = jnp.where(columns < width_ref[0], pooled, 0.0).astype(BF16)


def pool_local(lookup, lengths, embedding, own_width, first_column):
    samples, bag = lookup.shape
    vocab, columns = embedding.shape
    low, group = 256, 16
    high = vocab // low
    in_bag = jnp.arange(bag)[None, :] < lengths[:, None]
    sample_in_group = (jnp.arange(samples) % group)[:, None]
    hi_key = jnp.where(in_bag, (lookup // low) * group + sample_in_group, -1)
    lo_key = lookup % low
    return pl.pallas_call(
        functools.partial(pool_kernel, group=group, low=low),
        out_shape=jax.ShapeDtypeStruct((samples, columns), BF16),
        in_specs=[pl.BlockSpec(memory_space=pltpu.SMEM)] + [pl.BlockSpec(memory_space=pltpu.VMEM)] * 4,
        out_specs=pl.BlockSpec(memory_space=pltpu.VMEM),
        scratch_shapes=[pltpu.VMEM((high, samples, low), BF16)],
        compiler_params=params(48),
        name="pool",
    )(
        jnp.stack([own_width, first_column]).astype(jnp.int32),
        hi_key.reshape(samples // group, group * bag),
        lo_key.reshape(samples // group, group * bag),
        lengths[:, None],
        embedding,
    )


def place_kernel(place_ref, own_ref, other_ref, out_ref):
    j = pl.program_id(1)
    half = pl.num_programs(1) // 2

    @pl.when(j < half)
    def _():
        out_ref[...] = own_ref[0]

    @pl.when(j >= half)
    def _():
        out_ref[...] = other_ref[0]


def place_features(place, own, other):
    half, chunks, samples, columns = own.shape
    slots = 2 * half
    return pl.pallas_call(
        place_kernel,
        out_shape=jax.ShapeDtypeStruct((chunks, samples, slots * columns), BF16),
        grid_spec=pltpu.PrefetchScalarGridSpec(
            num_scalar_prefetch=1,
            grid=(chunks, slots),
            in_specs=[
                pl.BlockSpec((1, 1, samples, columns), lambda k, j, p: (jnp.minimum(j, half - 1), k, 0, 0)),
                pl.BlockSpec((1, 1, samples, columns), lambda k, j, p: (jnp.maximum(j - half, 0), k, 0, 0)),
            ],
            out_specs=pl.BlockSpec((1, samples, columns), lambda k, j, p: (k, 0, p[j])),
        ),
        compiler_params=params(32),
        name="place_features",
    )(place, own, other)


def hidden_kernel(feat_ref, w_ref, out_ref):
    preact = jnp.dot(feat_ref[...], w_ref[...], preferred_element_type=F32)
    out_ref[...] = jax.nn.silu(preact).astype(BF16)


def hidden_of(feat, w_in):
    samples, depth = feat.shape
    units = w_in.shape[1]
    wide = min(units, 512)
    return pl.pallas_call(
        hidden_kernel,
        out_shape=jax.ShapeDtypeStruct((samples, units), BF16),
        grid=(units // wide,),
        in_specs=[
            pl.BlockSpec((samples, depth), lambda i: (0, 0)),
            pl.BlockSpec((depth, wide), lambda i: (0, i)),
        ],
        out_specs=pl.BlockSpec((samples, wide), lambda i: (0, i)),
        compiler_params=params(48),
        name="hidden",
    )(feat, w_in)


def mixed_kernel(place_ref, hidden_ref, w_ref, out_ref):
    product = jnp.dot(hidden_ref[...], w_ref[...], preferred_element_type=F32)
    out_ref[0] = product.astype(out_ref.dtype)


def mixed_blocks(place, hidden, w_out, wide, dtype):
    samples, units = hidden.shape
    slots = place.shape[0]
    return pl.pallas_call(
        mixed_kernel,
        out_shape=jax.ShapeDtypeStruct((slots, samples, wide), dtype),
        grid_spec=pltpu.PrefetchScalarGridSpec(
            num_scalar_prefetch=1,
            grid=(slots,),
            in_specs=[
                pl.BlockSpec((samples, units), lambda j, p: (0, 0)),
                pl.BlockSpec((units, wide), lambda j, p: (0, p[j])),
            ],
            out_specs=pl.BlockSpec((1, samples, wide), lambda j, p: (j, 0, 0)),
        ),
        compiler_params=params(48),
        name="mixed",
    )(place, hidden, w_out)


def chunk_kernel(
    place_ref, own_ref, other_ref, w_out_ref, feat_ref, w_in_ref, sum_ref,
    hidden_ref, grad_in_ref, grad_hidden_ref,
):
    j = pl.program_id(0)
    slots = pl.num_programs(0)
    half = slots // 2

    @pl.when(j == 0)
    def _():
        grad_hidden_ref[...] = jnp.zeros_like(grad_hidden_ref)

    @pl.when(j < half)
    def _():
        grad_hidden_ref[...] += lax.dot_general(
            own_ref[0], w_out_ref[...], COLS_NT, preferred_element_type=F32
        )

    @pl.when(j >= half)
    def _():
        grad_hidden_ref[...] += lax.dot_general(
            other_ref[0], w_out_ref[...], COLS_NT, preferred_element_type=F32
        )

    @pl.when(j == slots - 1)
    def _():
        preact = jnp.dot(feat_ref[0], w_in_ref[...], preferred_element_type=F32)
        hidden_ref[...] = jax.nn.silu(preact).astype(BF16)
        grad_preact = (grad_hidden_ref[...] * silu_slope(preact)).astype(BF16)
        grad_in_ref[...] = sum_ref[...] + lax.dot_general(
            feat_ref[0], grad_preact, ROWS_TN, preferred_element_type=F32
        )


def chunk_backward(place, own, other, w_out, features, w_in, chunk, running, units):
    half, samples, wide = own.shape
    slots = 2 * half
    depth = w_in.shape[0]
    return pl.pallas_call(
        chunk_kernel,
        out_shape=(
            jax.ShapeDtypeStruct((samples, units), BF16),
            jax.ShapeDtypeStruct((depth, units), F32),
        ),
        grid_spec=pltpu.PrefetchScalarGridSpec(
            num_scalar_prefetch=1,
            grid=(slots,),
            in_specs=[
                pl.BlockSpec((1, samples, wide), lambda j, p: (jnp.minimum(j, half - 1), 0, 0)),
                pl.BlockSpec((1, samples, wide), lambda j, p: (jnp.maximum(j - half, 0), 0, 0)),
                pl.BlockSpec((units, wide), lambda j, p: (p[slots], p[j])),
                pl.BlockSpec((1, samples, depth), lambda j, p: (chunk, 0, 0)),
                pl.BlockSpec((depth, units), lambda j, p: (0, p[slots])),
                pl.BlockSpec((depth, units), lambda j, p: (0, 0)),
            ],
            out_specs=[
                pl.BlockSpec((samples, units), lambda j, p: (0, 0)),
                pl.BlockSpec((depth, units), lambda j, p: (0, 0)),
            ],
            scratch_shapes=[pltpu.VMEM((samples, units), F32)],
        ),
        compiler_params=params(48),
        name="chunk_backward",
    )(place, own, other, w_out, features, w_in, running)


def grad_out_kernel(place_ref, *refs):
    chunks = (len(refs) - 2) // 3
    hidden, own, other = refs[:chunks], refs[chunks : 2 * chunks], refs[2 * chunks : 3 * chunks]
    out_ref, turned_ref = refs[3 * chunks :]
    j = pl.program_id(0)
    half = pl.num_programs(0) // 2
    samples = hidden[0].shape[0]

    @pl.when(j == 0)
    def _():
        for k in range(chunks):
            turned_ref[:, k * samples : (k + 1) * samples] = hidden[k][...].T

    def product(blocks):
        total = None
        for k in range(chunks):
            term = jnp.dot(
                turned_ref[:, k * samples : (k + 1) * samples], blocks[k][0], preferred_element_type=F32
            )
            total = term if total is None else total + term
        out_ref[...] = total

    @pl.when(j < half)
    def _():
        product(own)

    @pl.when(j >= half)
    def _():
        product(other)


def grad_out_of(place, hidden, own, other):
    chunks = len(hidden)
    samples, units = hidden[0].shape
    half, unused, wide = own[0].shape
    slots = 2 * half
    return pl.pallas_call(
        grad_out_kernel,
        out_shape=jax.ShapeDtypeStruct((units, slots * wide), F32),
        grid_spec=pltpu.PrefetchScalarGridSpec(
            num_scalar_prefetch=1,
            grid=(slots,),
            in_specs=[pl.BlockSpec((samples, units), lambda j, p: (0, 0))] * chunks
            + [pl.BlockSpec((1, samples, wide), lambda j, p: (jnp.minimum(j, half - 1), 0, 0))] * chunks
            + [pl.BlockSpec((1, samples, wide), lambda j, p: (jnp.maximum(j - half, 0), 0, 0))] * chunks,
            out_specs=pl.BlockSpec((units, wide), lambda j, p: (0, p[j])),
            scratch_shapes=[pltpu.VMEM((units, chunks * samples), BF16)],
        ),
        compiler_params=params(56),
        name="grad_out",
    )(place, *hidden, *own, *other)


def plane_perms():
    first, second = [], []
    for t in range(4):
        for y in range(2):
            along_x, along_y = (t ^ 2) * 2 + y, t * 2 + (y ^ 1)
            first.append((t * 2 + y, along_x if t % 2 == 0 else along_y))
            second.append((t * 2 + y, along_y if t % 2 == 0 else along_x))
    return first, second


PERM_A, PERM_B = plane_perms()


def move_a(v):
    return lax.ppermute(v, PLANE, PERM_A)


def move_b(v):
    return lax.ppermute(v, PLANE, PERM_B)


def swap(v):
    return lax.ppermute(v, "table", [(t, t ^ 1) for t in range(4)])


def move_z(v, k):
    return lax.ppermute(v, "dp", [(z, z ^ k) for z in range(4)])


def plane_blocks():
    t, y = lax.axis_index("table"), lax.axis_index("tensor")
    x, core = t // 2, t % 2
    blocks = []
    for dc in range(2):
        c = core ^ dc
        a_x, a_y = jnp.where(c == 0, 1, 0), jnp.where(c == 0, 0, 1)
        for dx, dy in ((0, 0), (a_x, a_y), (a_y, a_x), (1, 1)):
            blocks.append(((x ^ dx) * 2 + c) * 2 + (y ^ dy))
    return jnp.stack(blocks).astype(jnp.int32)


def spread_shards(lookup_ids, bag_lengths, feature_widths, tables, w_in, w_out, cotangent):
    embedding = tables[0]
    half_width = embedding.shape[1]
    z = lax.axis_index("dp")
    samples, wide = cotangent.shape
    units = w_in.shape[1] // 4
    blocks = plane_blocks()
    place = jnp.concatenate([blocks, z[None].astype(jnp.int32)])

    s0 = cotangent
    a0, b0 = move_a(s0), move_b(s0)
    s2 = move_z(s0, 2)

    own_width = lax.dynamic_index_in_dim(feature_widths, lax.axis_index("table"), 0, keepdims=False)
    pooled = pool_local(
        lookup_ids[:, 0, :], bag_lengths[:, 0], embedding, own_width, lax.axis_index("tensor") * half_width
    )
    p_all = jnp.stack([pooled] + [move_z(pooled, k) for k in (1, 2, 3)])
    pa, pb = move_a(p_all), move_b(p_all)
    pd = move_b(pa)
    own_feat = jnp.stack([p_all, pa, pb, pd])
    features = place_features(blocks, own_feat, swap(own_feat))

    d0 = move_b(a0)
    own0 = jnp.stack([s0, a0, b0, d0])
    own1 = move_z(own0, 1)
    a2, b2 = move_a(s2), move_b(s2)
    own2 = jnp.stack([s2, a2, b2, move_b(a2)])
    s3 = move_z(s0, 3)
    a3, b3 = move_a(s3), move_b(s3)
    own3 = jnp.stack([s3, a3, b3, move_b(a3)])
    own = [own0, own1, own2, own3]
    other = [swap(v) for v in own]

    hidden_here = hidden_of(features[0], w_in)
    away = mixed_blocks(blocks[4:], hidden_here, w_out, wide, BF16)
    near = mixed_blocks(blocks[:4], hidden_here, w_out, wide, F32)
    near = near + swap(away).astype(F32)
    to_a = near[1] + move_b(near[3].astype(BF16)).astype(F32)
    mixed_out = near[0] + move_b(near[2].astype(BF16)).astype(F32)
    mixed_out = (mixed_out + move_a(to_a.astype(BF16)).astype(F32)).astype(BF16)

    hidden = [None] * 4
    running = jnp.zeros((w_in.shape[0], units), F32)
    for k in (0, 2, 1, 3):
        hidden[k], running = chunk_backward(
            place, own[k], other[k], w_out, features, w_in, k, running, units
        )
    rows = w_in.shape[0] // 4
    grad_in = jnp.zeros((rows, 4 * units), F32)
    for k in range(4):
        part = lax.dynamic_slice_in_dim(running, (z ^ k) * rows, rows, 0)
        part = part if k == 0 else move_z(part.astype(BF16), k).astype(F32)
        grad_in = lax.dynamic_update_slice_in_dim(grad_in, part, (z ^ k) * units, 1)
    grad_out = grad_out_of(blocks, hidden, own, other)
    return (mixed_out, grad_in, grad_out)


def summed_shards(lookup_ids, bag_lengths, feature_widths, tables, w_in, w_out, cotangent):
    embedding = tables[0]
    half_width = embedding.shape[1]
    own_width = lax.dynamic_index_in_dim(feature_widths, lax.axis_index("table"), 0, keepdims=False)
    pooled = pool_local(
        lookup_ids[:, 0, :], bag_lengths[:, 0], embedding, own_width, lax.axis_index("tensor") * half_width
    )
    features = lax.all_gather(pooled, PLANE, axis=1, tiled=True)
    preact = jnp.dot(features, w_in, preferred_element_type=F32)
    hidden = jax.nn.silu(preact).astype(BF16)
    partial_out = jnp.dot(hidden, w_out, preferred_element_type=F32)
    reduced = lax.psum_scatter(partial_out, PLANE, scatter_dimension=1, tiled=True)
    mixed_out = reduced.astype(BF16)
    whole_grad = lax.all_gather(cotangent, PLANE, axis=1, tiled=True)
    grad_hidden = lax.dot_general(whole_grad, w_out, COLS_NT, preferred_element_type=F32)
    grad_preact = (grad_hidden * silu_slope(preact)).astype(BF16)
    term_in = lax.dot_general(features, grad_preact, ROWS_TN, preferred_element_type=F32)
    term_out = lax.dot_general(hidden, whole_grad, ROWS_TN, preferred_element_type=F32)
    grad_in = lax.psum_scatter(term_in, "dp", scatter_dimension=0, tiled=True)
    grad_out = lax.psum_scatter(term_out, "dp", scatter_dimension=0, tiled=True)
    return (mixed_out, grad_in, grad_out)


def solution(mesh):
    sizes = (mesh.shape["table"], mesh.shape["tensor"], mesh.shape["dp"])
    return jax.shard_map(
        spread_shards if sizes == (4, 2, 4) else summed_shards,
        mesh=mesh,
        in_specs=(
            P("dp", "table", None),
            P("dp", "table"),
            P(),
            P("table", None, "tensor"),
            P(None, PLANE),
            P(PLANE, None),
            P("dp", PLANE),
        ),
        out_specs=(
            P("dp", PLANE),
            P("dp", PLANE),
            P(("table", "tensor", "dp"), None),
        ),
        check_vma=False,
    )
```

```python
import functools

import jax
import jax.numpy as jnp
from jax import lax
from jax.experimental import pallas as pl
from jax.experimental.pallas import tpu as pltpu
from jax.sharding import PartitionSpec as P

F32 = jnp.float32
BF16 = jnp.bfloat16
PLANE = ("table", "tensor")
ROWS_TN = (((0,), (0,)), ((), ()))
COLS_NT = (((1,), (1,)), ((), ()))


def silu_slope(preact):
    sigmoid_part = jax.nn.sigmoid(preact)
    return sigmoid_part * (1.0 + preact * (1.0 - sigmoid_part))


def cost(flops, bytes_accessed, transcendentals):
    return pl.CostEstimate(flops=flops, bytes_accessed=bytes_accessed, transcendentals=transcendentals)


def params(mib):
    return pltpu.CompilerParams(vmem_limit_bytes=mib * 1024 * 1024)


def pool_kernel(key_ref, len_ref, width_ref, table_ref, out_ref, counts_ref, *, group, low):
    samples, columns = out_ref.shape
    slots = key_ref.shape[1]
    bag = slots // group
    high = table_ref.shape[0] // low
    rows = lax.broadcasted_iota(jnp.int32, (high * group, slots), 0)
    low_rows = lax.broadcasted_iota(jnp.int32, (low, slots), 0)
    lane = lax.broadcasted_iota(jnp.int32, (1, slots), 1)
    member, slot = lane // bag, lax.rem(lane, bag)
    group_rows = lax.broadcasted_iota(jnp.int32, (group, slots), 0)

    def one_group(g, carry):
        first = pl.multiple_of(g * group, group)
        lengths = jnp.where(group_rows == member, len_ref[pl.ds(first, group), :], 0)
        in_bag = slot < jnp.sum(lengths, axis=0, keepdims=True)
        key = key_ref[pl.ds(g, 1), :]
        hit_high = (rows == jnp.where(in_bag, (key // low) * group + member, -1)).astype(BF16)
        hit_low = (low_rows == lax.rem(key, low)).astype(BF16)
        counts = lax.dot_general(hit_high, hit_low, COLS_NT, preferred_element_type=F32).astype(BF16)
        for h in range(high):
            counts_ref[h, pl.ds(first, group), :] = counts[h * group : (h + 1) * group, :]
        return carry

    lax.fori_loop(0, samples // group, one_group, 0, unroll=4)
    total = jnp.zeros(out_ref.shape, F32)
    for h in range(high):
        total += jnp.dot(
            counts_ref[h], table_ref[h * low : (h + 1) * low, :], preferred_element_type=F32
        )
    pooled = total / len_ref[...].astype(F32)
    position = lax.axis_index("tensor") * columns + lax.broadcasted_iota(jnp.int32, pooled.shape, 1)
    out_ref[...] = jnp.where(position < width_ref[lax.axis_index("table")], pooled, 0.0).astype(BF16)


def pool_local(lookup_ids, bag_lengths, feature_widths, embedding):
    samples, unused, bag = lookup_ids.shape
    vocab, columns = embedding.shape
    low, group = 256, 16
    high = vocab // low
    return pl.pallas_call(
        functools.partial(pool_kernel, group=group, low=low),
        out_shape=jax.ShapeDtypeStruct((samples, columns), BF16),
        in_specs=[
            pl.BlockSpec(memory_space=pltpu.VMEM),
            pl.BlockSpec(memory_space=pltpu.VMEM),
            pl.BlockSpec(memory_space=pltpu.SMEM),
            pl.BlockSpec(memory_space=pltpu.VMEM),
        ],
        out_specs=pl.BlockSpec(memory_space=pltpu.VMEM),
        scratch_shapes=[pltpu.VMEM((high, samples, low), BF16)],
        compiler_params=params(56),
        cost_estimate=cost(4 * samples * vocab * columns, 2 * vocab * columns, 0),
        name="pool",
    )(lookup_ids.reshape(samples // group, group * bag), bag_lengths, feature_widths, embedding)


def block_copies(place_ref, refs, first, width, buffer, sem, in_place):
    copies = []
    each = 8 // len(refs)
    for j in range(8):
        to = pl.multiple_of(place_ref[j] * width, width) if in_place else j * width
        source = refs[j // each].at[j % each, :, pl.ds(first, width)]
        copies.append(pltpu.make_async_copy(source, buffer.at[:, pl.ds(to, width)], sem.at[j]))
    return copies


def start_all(copies):
    for c in copies:
        c.start()


def wait_all(copies):
    for c in copies:
        c.wait()


def hidden_kernel(place_ref, blocks_ref, w_in_ref, hidden_ref, feat_ref, sem, *, step):
    copies = block_copies(place_ref, [blocks_ref], 0, blocks_ref.shape[2], feat_ref, sem, True)
    start_all(copies)
    wait_all(copies)
    for i in range(hidden_ref.shape[1] // step):
        here = slice(i * step, (i + 1) * step)
        preact = jnp.dot(feat_ref[...], w_in_ref[:, here], preferred_element_type=F32)
        hidden_ref[:, here] = jax.nn.silu(preact).astype(BF16)


def hidden_of(place, feat_blocks, w_in):
    samples = feat_blocks.shape[1]
    depth, units = w_in.shape
    in_vmem = pl.BlockSpec(memory_space=pltpu.VMEM)
    return pl.pallas_call(
        functools.partial(hidden_kernel, step=512),
        out_shape=jax.ShapeDtypeStruct((samples, units), BF16),
        in_specs=[pl.BlockSpec(memory_space=pltpu.SMEM), pl.BlockSpec(memory_space=pl.ANY), in_vmem],
        out_specs=in_vmem,
        scratch_shapes=[pltpu.VMEM((samples, depth), BF16), pltpu.SemaphoreType.DMA((8,))],
        compiler_params=params(56),
        cost_estimate=cost(2 * samples * units * depth, 2 * units * depth, samples * units),
        name="hidden",
    )(place, feat_blocks, w_in)


def mixed_kernel(place_ref, hidden_ref, w_ref, out_ref):
    out_ref[0] = jnp.dot(hidden_ref[...], w_ref[...], preferred_element_type=F32).astype(out_ref.dtype)


def mixed_blocks(place, hidden, w_out, wide, dtype):
    samples, units = hidden.shape
    slots = place.shape[0]
    return pl.pallas_call(
        mixed_kernel,
        out_shape=jax.ShapeDtypeStruct((slots, samples, wide), dtype),
        grid_spec=pltpu.PrefetchScalarGridSpec(
            num_scalar_prefetch=1,
            grid=(slots,),
            in_specs=[
                pl.BlockSpec((samples, units), lambda j, p: (0, 0)),
                pl.BlockSpec((units, wide), lambda j, p: (0, p[j])),
            ],
            out_specs=pl.BlockSpec((1, samples, wide), lambda j, p: (j, 0, 0)),
        ),
        compiler_params=params(56),
        cost_estimate=cost(2 * samples * units * slots * wide, 2 * units * slots * wide, 0),
        name="mixed",
    )(place, hidden, w_out)


def chunk_kernel(place_ref, *refs, wide, first, feats):
    cot_refs, feat_refs = refs[:4], refs[4 : 4 + feats]
    w_out_ref, w_in_ref, sum_ref, hidden_ref, grad_in_ref = refs[4 + feats : 9 + feats]
    cot_buf, w_out_buf, feat_buf, w_in_buf, sum_buf, cot_sem, w_sem, feat_sem, sem = refs[9 + feats :]
    units = hidden_ref.shape[0]
    row = pl.ds(pl.multiple_of(place_ref[8] * units, units), units)
    cot_copies = block_copies(place_ref, cot_refs, 0, wide, cot_buf, cot_sem, False)
    w_copies = []
    for j in range(8):
        column = pl.ds(pl.multiple_of(place_ref[j] * wide, wide), wide)
        w_copies.append(
            pltpu.make_async_copy(w_out_ref.at[row, column], w_out_buf.at[:, pl.ds(j * wide, wide)], w_sem.at[j])
        )
    feat_copies = block_copies(place_ref, feat_refs, first, feat_buf.shape[1] // 8, feat_buf, feat_sem, True)
    w_in_copy = pltpu.make_async_copy(w_in_ref.at[:, row], w_in_buf, sem.at[0])
    sum_copy = pltpu.make_async_copy(sum_ref, sum_buf, sem.at[1])
    start_all(feat_copies)
    w_in_copy.start()
    start_all(cot_copies[:4] + w_copies[:4])
    start_all(cot_copies[4:] + w_copies[4:])
    sum_copy.start()

    wait_all(feat_copies)
    w_in_copy.wait()
    preact = jnp.dot(feat_buf[...], w_in_buf[...], preferred_element_type=F32)
    hidden_ref[...] = jax.nn.silu(preact).astype(BF16).T
    slope = silu_slope(preact)
    middle = 4 * wide
    wait_all(cot_copies[:4] + w_copies[:4])
    grad_hidden = lax.dot_general(
        cot_buf[:, :middle], w_out_buf[:, :middle], COLS_NT, preferred_element_type=F32
    )
    wait_all(cot_copies[4:] + w_copies[4:])
    grad_hidden += lax.dot_general(
        cot_buf[:, middle:], w_out_buf[:, middle:], COLS_NT, preferred_element_type=F32
    )
    grad_preact = (grad_hidden * slope).astype(BF16)
    sum_copy.wait()
    grad_in_ref[...] = sum_buf[...] + lax.dot_general(
        feat_buf[...], grad_preact, ROWS_TN, preferred_element_type=F32
    )


def chunk_backward(place, cot_blocks, feat_blocks, first, w_out, w_in, running, wide):
    samples = cot_blocks[0].shape[1]
    depth, units = running.shape
    any_space = pl.BlockSpec(memory_space=pl.ANY)
    in_vmem = pl.BlockSpec(memory_space=pltpu.VMEM)
    return pl.pallas_call(
        functools.partial(chunk_kernel, wide=wide, first=first, feats=len(feat_blocks)),
        out_shape=(
            jax.ShapeDtypeStruct((units, samples), BF16),
            jax.ShapeDtypeStruct((depth, units), F32),
        ),
        in_specs=[pl.BlockSpec(memory_space=pltpu.SMEM)] + [any_space] * (7 + len(feat_blocks)),
        out_specs=(in_vmem, in_vmem),
        scratch_shapes=[
            pltpu.VMEM((samples, 8 * wide), BF16),
            pltpu.VMEM((units, 8 * wide), BF16),
            pltpu.VMEM((samples, depth), BF16),
            pltpu.VMEM((depth, units), BF16),
            pltpu.VMEM((depth, units), F32),
            pltpu.SemaphoreType.DMA((8,)),
            pltpu.SemaphoreType.DMA((8,)),
            pltpu.SemaphoreType.DMA((8,)),
            pltpu.SemaphoreType.DMA((2,)),
        ],
        compiler_params=params(56),
        cost_estimate=cost(
            2 * samples * units * (8 * wide + 2 * depth),
            2 * (samples + units) * (8 * wide + depth) + 8 * depth * units,
            2 * samples * units,
        ),
        name="chunk_backward",
    )(place, *cot_blocks, *feat_blocks, w_out, w_in, running)


def grad_out_kernel(place_ref, *refs, chunks):
    hidden, blocks = refs[:chunks], refs[chunks : 5 * chunks]
    out_ref, hidden_buf, cot_buf, hidden_sem, cot_sem = refs[5 * chunks :]
    samples, wide = hidden[0].shape[1], out_ref.shape[1]
    j = pl.program_id(0)
    rows = [slice(k * samples, (k + 1) * samples) for k in range(chunks)]

    def fetch(slot, action):
        buffer = lax.rem(slot, 2)
        for i in range(4):

            @pl.when(slot // 2 == i)
            def _():
                for k in range(chunks):
                    source = blocks[4 * k + i].at[lax.rem(slot, 2), :, pl.ds(0, wide)]
                    action(pltpu.make_async_copy(source, cot_buf.at[buffer, rows[k]], cot_sem.at[buffer, k]))

    hidden_copies = [
        pltpu.make_async_copy(hidden[k], hidden_buf.at[:, rows[k]], hidden_sem.at[k]) for k in range(chunks)
    ]

    @pl.when(j == 0)
    def _():
        start_all(hidden_copies)
        fetch(j, lambda c: c.start())

    @pl.when(j + 1 < pl.num_programs(0))
    def _():
        fetch(j + 1, lambda c: c.start())

    @pl.when(j == 0)
    def _():
        wait_all(hidden_copies)

    fetch(j, lambda c: c.wait())
    out_ref[...] = jnp.dot(hidden_buf[...], cot_buf[lax.rem(j, 2)], preferred_element_type=F32)


def grad_out_of(place, hidden, cot_blocks, wide):
    chunks = len(hidden)
    units, samples = hidden[0].shape
    flat = [array for blocks in cot_blocks for array in blocks]
    return pl.pallas_call(
        functools.partial(grad_out_kernel, chunks=chunks),
        out_shape=jax.ShapeDtypeStruct((units, 8 * wide), F32),
        grid_spec=pltpu.PrefetchScalarGridSpec(
            num_scalar_prefetch=1,
            grid=(8,),
            in_specs=[pl.BlockSpec(memory_space=pl.ANY)] * (5 * chunks),
            out_specs=pl.BlockSpec((units, wide), lambda j, p: (0, p[j])),
            scratch_shapes=[
                pltpu.VMEM((units, chunks * samples), BF16),
                pltpu.VMEM((2, chunks * samples, wide), BF16),
                pltpu.SemaphoreType.DMA((chunks,)),
                pltpu.SemaphoreType.DMA((2, chunks)),
            ],
        ),
        compiler_params=params(56),
        cost_estimate=cost(
            2 * units * chunks * samples * 8 * wide,
            2 * chunks * samples * (8 * wide + units) + 4 * units * 8 * wide,
            0,
        ),
        name="grad_out",
    )(place, *hidden, *flat)


def plane_perms():
    first, second = [], []
    for t in range(4):
        for y in range(2):
            along_x, along_y = (t ^ 2) * 2 + y, t * 2 + (y ^ 1)
            first.append((t * 2 + y, along_x if t % 2 == 0 else along_y))
            second.append((t * 2 + y, along_y if t % 2 == 0 else along_x))
    return first, second


PERM_A, PERM_B = plane_perms()


def move_a(v):
    return lax.ppermute(v, PLANE, PERM_A)


def move_b(v):
    return lax.ppermute(v, PLANE, PERM_B)


def swap(v):
    return lax.ppermute(v, "table", [(t, t ^ 1) for t in range(4)])


def move_z(v, k):
    return lax.ppermute(v, "dp", [(z, z ^ k) for z in range(4)])


def plane_blocks():
    t, y = lax.axis_index("table"), lax.axis_index("tensor")
    x, core = t // 2, t % 2
    blocks = []
    for dc in range(2):
        c = core ^ dc
        a_x, a_y = jnp.where(c == 0, 1, 0), jnp.where(c == 0, 0, 1)
        for dx, dy in ((0, 0), (a_x, a_y), (a_y, a_x), (1, 1)):
            blocks.append(((x ^ dx) * 2 + c) * 2 + (y ^ dy))
    return jnp.stack(blocks).astype(jnp.int32)


def after(v, *earlier):
    return lax.optimization_barrier((v,) + earlier)[0]


def spread_shards(lookup_ids, bag_lengths, feature_widths, tables, w_in, w_out, cotangent):
    z = lax.axis_index("dp")
    wide = cotangent.shape[1]
    units = w_in.shape[1] // 4
    blocks = plane_blocks()
    place = jnp.concatenate([blocks, z[None].astype(jnp.int32)])

    def backward(cot, feat, first, running):
        return chunk_backward(place, cot, feat, first, w_out, w_in, running, wide)

    s0 = cotangent
    a0 = move_a(s0)
    s1, s2 = move_z(s0, 1), move_z(s0, 2)
    pair0 = jnp.stack([s0, a0])
    both0 = move_b(pair0)
    pair0_ = swap(pair0)
    pooled = pool_local(lookup_ids, bag_lengths, after(feature_widths, pair0), tables[0])
    pa = move_a(pooled)
    pooled1, pooled2 = move_z(pooled, 1), move_z(pooled, 2)
    feat_pair = jnp.stack([pooled, after(pa, both0)])
    both0_ = swap(both0)
    feat_both = move_b(feat_pair)

    e1 = jnp.concatenate([after(s1, feat_pair), after(pooled1, feat_pair)], axis=1)
    a1 = move_a(e1)
    e2 = jnp.concatenate([after(s2, e1), after(pooled2, e1)], axis=1)
    e3 = move_z(e2, 1)
    feat0 = jnp.concatenate([feat_pair, feat_both, swap(feat_pair), swap(feat_both)])
    hidden_here = hidden_of(blocks, after(feat0, e2), w_in)

    pair1 = jnp.stack([e1, after(a1, hidden_here)])
    both1, a2 = move_b(pair1), move_a(after(e2, pair1))
    pair1_ = swap(pair1)
    away = mixed_blocks(blocks[4:], after(hidden_here, pair1, both0_), w_out, wide, BF16)
    got = swap(away)
    near = mixed_blocks(blocks[:4], after(hidden_here, away), w_out, wide, F32)

    pair2 = jnp.stack([e2, after(a2, near)])
    both1 = after(both1, pair2)
    both1_ = swap(both1)
    both2, a3 = move_b(pair2), move_a(after(e3, pair2))
    pair2_ = swap(pair2)
    running = jnp.zeros((w_in.shape[0], units), F32)
    cot0 = [pair0, both0, pair0_, both0_]
    hidden0, running = backward(cot0, [feat0], 0, after(running, pair2))
    cot1 = [pair1, both1, pair1_, both1_]
    hidden1, running = backward(cot1, cot1, wide, running)

    pair3 = jnp.stack([e3, after(a3, running)])
    both2 = after(both2, pair3)
    both2_ = swap(both2)
    both3 = move_b(pair3)
    pair3_ = swap(pair3)
    near = near + after(got, pair3).astype(F32)
    cot2 = [pair2, both2, pair2_, both2_]
    hidden2, running = backward(cot2, cot2, wide, after(running, near))

    both3 = after(both3, running)
    both3_ = swap(both3)
    moved = move_b(after(near, both3)[2:].astype(BF16))
    cot3 = [pair3, both3, pair3_, both3_]
    hidden3, running = backward(cot3, cot3, wide, running)
    moved = after(moved, running).astype(F32)
    last = move_a((near[1] + moved[1]).astype(BF16))

    rows = w_in.shape[0] // 4
    grad_in = jnp.zeros((rows, 4 * units), F32)
    for k in range(4):
        part = lax.dynamic_slice_in_dim(running, (z ^ k) * rows, rows, 0)
        part = part if k == 0 else move_z(part.astype(BF16), k).astype(F32)
        grad_in = lax.dynamic_update_slice_in_dim(grad_in, part, (z ^ k) * units, 1)
    grad_out = grad_out_of(blocks, [hidden0, hidden1, hidden2, hidden3], [cot0, cot1, cot2, cot3], wide)
    mixed_out = (near[0] + moved[0] + after(last, grad_out).astype(F32)).astype(BF16)
    return (mixed_out, grad_in, grad_out)


def summed_shards(lookup_ids, bag_lengths, feature_widths, tables, w_in, w_out, cotangent):
    pooled = pool_local(lookup_ids, bag_lengths, feature_widths, tables[0])
    features = lax.all_gather(pooled, PLANE, axis=1, tiled=True)
    preact = jnp.dot(features, w_in, preferred_element_type=F32)
    hidden = jax.nn.silu(preact).astype(BF16)
    partial_out = jnp.dot(hidden, w_out, preferred_element_type=F32)
    reduced = lax.psum_scatter(partial_out, PLANE, scatter_dimension=1, tiled=True)
    mixed_out = reduced.astype(BF16)
    whole_grad = lax.all_gather(cotangent, PLANE, axis=1, tiled=True)
    grad_hidden = lax.dot_general(whole_grad, w_out, COLS_NT, preferred_element_type=F32)
    grad_preact = (grad_hidden * silu_slope(preact)).astype(BF16)
    term_in = lax.dot_general(features, grad_preact, ROWS_TN, preferred_element_type=F32)
    term_out = lax.dot_general(hidden, whole_grad, ROWS_TN, preferred_element_type=F32)
    grad_in = lax.psum_scatter(term_in, "dp", scatter_dimension=0, tiled=True)
    grad_out = lax.psum_scatter(term_out, "dp", scatter_dimension=0, tiled=True)
    return (mixed_out, grad_in, grad_out)


def solution(mesh):
    sizes = (mesh.shape["table"], mesh.shape["tensor"], mesh.shape["dp"])
    return jax.shard_map(
        spread_shards if sizes == (4, 2, 4) else summed_shards,
        mesh=mesh,
        in_specs=(
            P("dp", "table", None),
            P("dp", "table"),
            P(),
            P("table", None, "tensor"),
            P(None, PLANE),
            P(PLANE, None),
            P("dp", PLANE),
        ),
        out_specs=(
            P("dp", PLANE),
            P("dp", PLANE),
            P(("table", "tensor", "dp"), None),
        ),
        check_vma=False,
    )
```

```python
import functools

import jax
import jax.numpy as jnp
from jax import lax
from jax.experimental import pallas as pl
from jax.experimental.pallas import tpu as pltpu
from jax.sharding import PartitionSpec as P

F32 = jnp.float32
BF16 = jnp.bfloat16
PLANE = ("table", "tensor")
VMEM_MIB = 50
ROWS_TN = (((0,), (0,)), ((), ()))
COLS_NT = (((1,), (1,)), ((), ()))


def silu_slope(preact):
    sigmoid_part = jax.nn.sigmoid(preact)
    return sigmoid_part * (1.0 + preact * (1.0 - sigmoid_part))


def cost(flops, bytes_accessed, transcendentals):
    return pl.CostEstimate(flops=flops, bytes_accessed=bytes_accessed, transcendentals=transcendentals)


def params(mib):
    return pltpu.CompilerParams(vmem_limit_bytes=mib * 1024 * 1024)


def pool_kernel(key_ref, len_ref, width_ref, table_ref, out_ref, counts_ref, *, group, low):
    samples, columns = out_ref.shape
    slots = key_ref.shape[1]
    bag = slots // group
    high = table_ref.shape[0] // low
    rows = lax.broadcasted_iota(jnp.int32, (high * group, slots), 0)
    low_rows = lax.broadcasted_iota(jnp.int32, (low, slots), 0)
    lane = lax.broadcasted_iota(jnp.int32, (1, slots), 1)
    member, slot = lane // bag, lax.rem(lane, bag)
    group_rows = lax.broadcasted_iota(jnp.int32, (group, slots), 0)

    def one_group(g, carry):
        first = pl.multiple_of(g * group, group)
        lengths = jnp.where(group_rows == member, len_ref[pl.ds(first, group), :], 0)
        in_bag = slot < jnp.sum(lengths, axis=0, keepdims=True)
        key = key_ref[pl.ds(g, 1), :]
        hit_high = (rows == jnp.where(in_bag, (key // low) * group + member, -1)).astype(BF16)
        hit_low = (low_rows == lax.rem(key, low)).astype(BF16)
        counts = lax.dot_general(hit_high, hit_low, COLS_NT, preferred_element_type=F32).astype(BF16)
        for h in range(high):
            counts_ref[h, pl.ds(first, group), :] = counts[h * group : (h + 1) * group, :]
        return carry

    lax.fori_loop(0, samples // group, one_group, 0, unroll=4)
    total = jnp.zeros(out_ref.shape, F32)
    for h in range(high):
        total += jnp.dot(
            counts_ref[h], table_ref[h * low : (h + 1) * low, :], preferred_element_type=F32
        )
    pooled = total / len_ref[...].astype(F32)
    position = lax.axis_index("tensor") * columns + lax.broadcasted_iota(jnp.int32, pooled.shape, 1)
    out_ref[...] = jnp.where(position < width_ref[lax.axis_index("table")], pooled, 0.0).astype(BF16)


def pool_local(lookup_ids, bag_lengths, feature_widths, embedding):
    samples, unused, bag = lookup_ids.shape
    vocab, columns = embedding.shape
    low, group = 256, 16
    high = vocab // low
    return pl.pallas_call(
        functools.partial(pool_kernel, group=group, low=low),
        out_shape=jax.ShapeDtypeStruct((samples, columns), BF16),
        in_specs=[
            pl.BlockSpec(memory_space=pltpu.VMEM),
            pl.BlockSpec(memory_space=pltpu.VMEM),
            pl.BlockSpec(memory_space=pltpu.SMEM),
            pl.BlockSpec(memory_space=pltpu.VMEM),
        ],
        out_specs=pl.BlockSpec(memory_space=pltpu.VMEM),
        scratch_shapes=[pltpu.VMEM((high, samples, low), BF16)],
        compiler_params=params(VMEM_MIB),
        cost_estimate=cost(20 * samples * vocab * columns, 2 * vocab * columns, 0),
        name="pool",
    )(lookup_ids.reshape(samples // group, group * bag), bag_lengths, feature_widths, embedding)


def carry_kernel(block_ref, feat_ref, out_ref):
    wide = block_ref.shape[1]
    out_ref[:, :wide] = block_ref[...]
    out_ref[:, wide:] = feat_ref[...]


def carry(block, feat, weight):
    in_vmem = pl.BlockSpec(memory_space=pltpu.VMEM)
    samples, wide = block.shape
    return pl.pallas_call(
        carry_kernel,
        out_shape=jax.ShapeDtypeStruct((samples, wide + feat.shape[1]), BF16),
        in_specs=[in_vmem, in_vmem],
        out_specs=in_vmem,
        cost_estimate=cost(weight * 10**9, 0, 0),
        name="carry",
    )(block, feat)


def block_copies(place_ref, refs, first, width, buffer, sem, in_place):
    copies = []
    each = 8 // len(refs)
    for j in range(8):
        to = pl.multiple_of(place_ref[j] * width, width) if in_place else j * width
        source = refs[j // each].at[j % each, :, pl.ds(first, width)]
        copies.append(pltpu.make_async_copy(source, buffer.at[:, pl.ds(to, width)], sem.at[j]))
    return copies


def start_all(copies):
    for c in copies:
        c.start()


def wait_all(copies):
    for c in copies:
        c.wait()


def forward_kernel(
    place_ref, feat_ref, other_feat_ref, w_in_ref, w_out_ref, away_ref, near_ref,
    feat_buf, w_in_buf, hidden_buf, w_out_buf, away_buf, near_buf,
    feat_sem, w_in_sem, w_out_sem, away_sem, near_sem,
):
    pieces, samples, step = w_in_buf.shape[0], hidden_buf.shape[0], w_in_buf.shape[2]
    buffers, wide = w_out_buf.shape[0], w_out_buf.shape[2]
    half = away_ref.shape[0]
    feat_copies = block_copies(
        place_ref, [feat_ref, other_feat_ref], 0, feat_ref.shape[2], feat_buf, feat_sem, True
    )
    w_in_copies = [
        pltpu.make_async_copy(w_in_ref.at[:, pl.ds(i * step, step)], w_in_buf.at[i], w_in_sem.at[i])
        for i in range(pieces)
    ]
    slots = [*range(half, 2 * half), *range(half)]
    w_out_copies = []
    for i, slot in enumerate(slots):
        column = pl.ds(pl.multiple_of(place_ref[slot] * wide, wide), wide)
        w_out_copies.append(
            pltpu.make_async_copy(w_out_ref.at[:, column], w_out_buf.at[i % buffers], w_out_sem.at[i % buffers])
        )
    start_all(feat_copies + w_in_copies + w_out_copies[: buffers - 1])
    wait_all(feat_copies)
    for i in range(pieces):
        w_in_copies[i].wait()
        preact = jnp.dot(feat_buf[...], w_in_buf[i], preferred_element_type=F32)
        hidden_buf[:, i * step : (i + 1) * step] = jax.nn.silu(preact).astype(BF16)
    out_copies = []
    for i in range(2 * half):
        if i + buffers - 1 < 2 * half:
            w_out_copies[i + buffers - 1].start()
        w_out_copies[i].wait()
        product = jnp.dot(hidden_buf[...], w_out_buf[i % buffers], preferred_element_type=F32)
        if i < half:
            away_buf[i] = product.astype(BF16)
            out_copies.append(pltpu.make_async_copy(away_buf.at[i], away_ref.at[i], away_sem.at[i]))
        else:
            near_buf[i - half] = product
            out_copies.append(pltpu.make_async_copy(near_buf.at[i - half], near_ref.at[i - half], near_sem.at[i - half]))
        out_copies[-1].start()
    wait_all(out_copies)


def forward(place, feat_blocks, w_in, w_out, wide):
    samples = feat_blocks[0].shape[1]
    depth, units = w_in.shape
    step, buffers = units // 4, 3
    any_space = pl.BlockSpec(memory_space=pl.ANY)
    return pl.pallas_call(
        forward_kernel,
        out_shape=(
            jax.ShapeDtypeStruct((4, samples, wide), BF16),
            jax.ShapeDtypeStruct((4, samples, wide), F32),
        ),
        in_specs=[pl.BlockSpec(memory_space=pltpu.SMEM)] + [any_space] * 4,
        out_specs=(any_space, any_space),
        scratch_shapes=[
            pltpu.VMEM((samples, depth), BF16),
            pltpu.VMEM((4, depth, step), BF16),
            pltpu.VMEM((samples, units), BF16),
            pltpu.VMEM((buffers, units, wide), BF16),
            pltpu.VMEM((4, samples, wide), BF16),
            pltpu.VMEM((4, samples, wide), F32),
            pltpu.SemaphoreType.DMA((8,)),
            pltpu.SemaphoreType.DMA((4,)),
            pltpu.SemaphoreType.DMA((buffers,)),
            pltpu.SemaphoreType.DMA((4,)),
            pltpu.SemaphoreType.DMA((4,)),
        ],
        compiler_params=params(VMEM_MIB),
        cost_estimate=cost(
            2 * samples * units * (depth + 8 * wide), 2 * units * (depth + 8 * wide), samples * units
        ),
        name="forward",
    )(place, *feat_blocks, w_in, w_out)


def chunk_kernel(place_ref, *refs, wide, firsts, feat_counts, add):
    chunks = len(firsts)
    cot_refs, refs = [refs[4 * k : 4 * k + 4] for k in range(chunks)], refs[4 * chunks :]
    feat_refs = []
    for n in feat_counts:
        feat_refs.append(refs[:n])
        refs = refs[n:]
    w_out_ref, w_in_ref, refs = refs[0], refs[1], refs[2:]
    sum_ref, refs = (refs[0], refs[1:]) if add else (None, refs)
    hidden_ref, grad_in_ref, cot_buf, w_out_buf, feat_buf, w_in_buf, sum_buf, cot_sem, w_sem, feat_sem, sem = refs
    units = hidden_ref.shape[0]
    samples = cot_buf.shape[0] // chunks
    row = pl.ds(pl.multiple_of(place_ref[8] * units, units), units)
    cot_copies, feat_copies, w_copies = [], [], []
    for k in range(chunks):
        rows = pl.ds(k * samples, samples)
        cot_copies.append(block_copies(place_ref, cot_refs[k], 0, wide, cot_buf.at[rows], cot_sem.at[k], False))
        feat_copies += block_copies(
            place_ref, feat_refs[k], firsts[k], feat_buf.shape[1] // 8, feat_buf.at[rows], feat_sem.at[k], True
        )
    for j in range(8):
        column = pl.ds(pl.multiple_of(place_ref[j] * wide, wide), wide)
        w_copies.append(
            pltpu.make_async_copy(w_out_ref.at[row, column], w_out_buf.at[:, pl.ds(j * wide, wide)], w_sem.at[j])
        )
    w_in_copy = pltpu.make_async_copy(w_in_ref.at[:, row], w_in_buf, sem.at[0])
    start_all(feat_copies)
    w_in_copy.start()
    early = [c for copies in cot_copies for c in copies[:4]] + w_copies[:4]
    late = [c for copies in cot_copies for c in copies[4:]] + w_copies[4:]
    start_all(early + late)
    if add:
        sum_copy = pltpu.make_async_copy(sum_ref, sum_buf, sem.at[1])
        sum_copy.start()

    wait_all(feat_copies)
    w_in_copy.wait()
    preact = jnp.dot(feat_buf[...], w_in_buf[...], preferred_element_type=F32)
    hidden_ref[...] = jax.nn.silu(preact).astype(BF16).T
    slope = silu_slope(preact)
    middle = 4 * wide
    wait_all(early)
    grad_hidden = lax.dot_general(
        cot_buf[:, :middle], w_out_buf[:, :middle], COLS_NT, preferred_element_type=F32
    )
    wait_all(late)
    grad_hidden += lax.dot_general(
        cot_buf[:, middle:], w_out_buf[:, middle:], COLS_NT, preferred_element_type=F32
    )
    grad_preact = (grad_hidden * slope).astype(BF16)
    term = lax.dot_general(feat_buf[...], grad_preact, ROWS_TN, preferred_element_type=F32)
    if add:
        sum_copy.wait()
        term += sum_buf[...]
    grad_in_ref[...] = term


def chunk_backward(place, cot, feat, firsts, w_out, w_in, running, units, wide):
    chunks = len(cot)
    samples = chunks * cot[0][0].shape[1]
    depth = w_in.shape[0]
    add = running is not None
    feat_counts = [len(f) for f in feat]
    operands = [v for c in cot for v in c] + [v for f in feat for v in f] + [w_out, w_in]
    operands += [running] if add else []
    in_vmem = pl.BlockSpec(memory_space=pltpu.VMEM)
    return pl.pallas_call(
        functools.partial(chunk_kernel, wide=wide, firsts=firsts, feat_counts=feat_counts, add=add),
        out_shape=(
            jax.ShapeDtypeStruct((units, samples), BF16),
            jax.ShapeDtypeStruct((depth, units), F32),
        ),
        in_specs=[pl.BlockSpec(memory_space=pltpu.SMEM)] + [pl.BlockSpec(memory_space=pl.ANY)] * len(operands),
        out_specs=(in_vmem, in_vmem),
        scratch_shapes=[
            pltpu.VMEM((samples, 8 * wide), BF16),
            pltpu.VMEM((units, 8 * wide), BF16),
            pltpu.VMEM((samples, depth), BF16),
            pltpu.VMEM((depth, units), BF16),
            pltpu.VMEM((depth, units) if add else (8, 128), F32),
            pltpu.SemaphoreType.DMA((chunks, 8)),
            pltpu.SemaphoreType.DMA((8,)),
            pltpu.SemaphoreType.DMA((chunks, 8)),
            pltpu.SemaphoreType.DMA((2,)),
        ],
        compiler_params=params(VMEM_MIB),
        cost_estimate=cost(
            2 * samples * units * (8 * wide + 2 * depth),
            2 * (samples + units) * (8 * wide + depth) + 8 * depth * units,
            2 * samples * units,
        ),
        name="chunk_backward",
    )(place, *operands)


def grad_out_kernel(place_ref, *refs, chunks):
    blocks, hidden = refs[: 4 * chunks], refs[4 * chunks : -5]
    out_ref, hidden_buf, cot_buf, hidden_sem, cot_sem = refs[-5:]
    samples, wide = cot_buf.shape[1] // chunks, out_ref.shape[1]
    j = pl.program_id(0)
    rows = [slice(k * samples, (k + 1) * samples) for k in range(chunks)]

    def fetch(slot, action):
        buffer = lax.rem(slot, 2)
        for i in range(4):

            @pl.when(slot // 2 == i)
            def _():
                for k in range(chunks):
                    source = blocks[4 * k + i].at[lax.rem(slot, 2), :, pl.ds(0, wide)]
                    action(pltpu.make_async_copy(source, cot_buf.at[buffer, rows[k]], cot_sem.at[buffer, k]))

    hidden_copies, first = [], 0
    for k, ref in enumerate(hidden):
        to = hidden_buf.at[:, pl.ds(first, ref.shape[1])]
        hidden_copies.append(pltpu.make_async_copy(ref, to, hidden_sem.at[k]))
        first += ref.shape[1]

    @pl.when(j == 0)
    def _():
        start_all(hidden_copies)
        fetch(j, lambda c: c.start())

    @pl.when(j + 1 < pl.num_programs(0))
    def _():
        fetch(j + 1, lambda c: c.start())

    @pl.when(j == 0)
    def _():
        wait_all(hidden_copies)

    fetch(j, lambda c: c.wait())
    out_ref[...] = jnp.dot(hidden_buf[...], cot_buf[lax.rem(j, 2)], preferred_element_type=F32)


def grad_out_of(place, hidden, cot_blocks, wide):
    chunks = len(cot_blocks)
    units, samples = hidden[0].shape[0], cot_blocks[0][0].shape[1]
    flat = [array for blocks in cot_blocks for array in blocks]
    return pl.pallas_call(
        functools.partial(grad_out_kernel, chunks=chunks),
        out_shape=jax.ShapeDtypeStruct((units, 8 * wide), F32),
        grid_spec=pltpu.PrefetchScalarGridSpec(
            num_scalar_prefetch=1,
            grid=(8,),
            in_specs=[pl.BlockSpec(memory_space=pl.ANY)] * (4 * chunks + len(hidden)),
            out_specs=pl.BlockSpec((units, wide), lambda j, p: (0, p[j])),
            scratch_shapes=[
                pltpu.VMEM((units, chunks * samples), BF16),
                pltpu.VMEM((2, chunks * samples, wide), BF16),
                pltpu.SemaphoreType.DMA((chunks,)),
                pltpu.SemaphoreType.DMA((2, chunks)),
            ],
        ),
        compiler_params=params(VMEM_MIB),
        cost_estimate=cost(
            2 * units * chunks * samples * 8 * wide,
            2 * chunks * samples * (8 * wide + units) + 4 * units * 8 * wide,
            0,
        ),
        name="grad_out",
    )(place, *flat, *hidden)


def plane_perms():
    first, second = [], []
    for t in range(4):
        for y in range(2):
            along_x, along_y = (t ^ 2) * 2 + y, t * 2 + (y ^ 1)
            first.append((t * 2 + y, along_x if t % 2 == 0 else along_y))
            second.append((t * 2 + y, along_y if t % 2 == 0 else along_x))
    return first, second


PERM_A, PERM_B = plane_perms()


def move_a(v):
    return lax.ppermute(v, PLANE, PERM_A)


def move_b(v):
    return lax.ppermute(v, PLANE, PERM_B)


def swap(v):
    return lax.ppermute(v, "table", [(t, t ^ 1) for t in range(4)])


def move_z(v, k):
    return lax.ppermute(v, "dp", [(z, z ^ k) for z in range(4)])


def plane_blocks():
    t, y = lax.axis_index("table"), lax.axis_index("tensor")
    x, core = t // 2, t % 2
    blocks = []
    for dc in range(2):
        c = core ^ dc
        a_x, a_y = jnp.where(c == 0, 1, 0), jnp.where(c == 0, 0, 1)
        for dx, dy in ((0, 0), (a_x, a_y), (a_y, a_x), (1, 1)):
            blocks.append(((x ^ dx) * 2 + c) * 2 + (y ^ dy))
    return jnp.stack(blocks).astype(jnp.int32)


def after(v, *earlier):
    return lax.optimization_barrier((v,) + earlier)[0]


def spread_shards(lookup_ids, bag_lengths, feature_widths, tables, w_in, w_out, cotangent):
    z = lax.axis_index("dp")
    wide = cotangent.shape[1]
    units = w_in.shape[1] // 4
    blocks = plane_blocks()
    place = jnp.concatenate([blocks, z[None].astype(jnp.int32)])

    def backward(cot, feat, firsts, running, *earlier):
        return chunk_backward(after(place, *earlier), cot, feat, firsts, w_out, w_in, running, units, wide)

    s0 = cotangent
    a0, s1, s2 = move_a(s0), move_z(s0, 1), move_z(s0, 2)
    pooled = pool_local(lookup_ids, bag_lengths, feature_widths, tables[0])
    pair0 = jnp.stack([s0, after(a0, pooled)])
    both0 = move_b(pair0)
    pa, pooled1 = move_a(pooled), move_z(pooled, 1)
    pa, pooled1, s1 = lax.optimization_barrier((pa, pooled1, s1))

    feat_pair = jnp.stack([pooled, pa])
    e1 = carry(s1, pooled1, 4)
    feat_pair, e1 = lax.optimization_barrier((feat_pair, e1))
    a1, feat_both, pooled2 = move_a(e1), move_b(feat_pair), move_z(after(pooled, e1), 2)
    s2, pooled2, both0 = lax.optimization_barrier((s2, pooled2, both0))
    e2 = carry(s2, pooled2, 6)
    feat0 = jnp.concatenate([feat_pair, after(feat_both, e2)])
    feat0_ = swap(feat0)
    pair1 = jnp.stack([e1, after(a1, feat0)])
    pair0_, both0_ = swap(after(pair0, pair1)), swap(after(both0, pair1))
    both1, pair1_ = move_b(pair1), swap(pair1)
    a2, e3 = move_a(after(e2, pair1)), move_z(e2, 1)
    away, near = forward(after(place, pair1, pair0_, both0_), [feat0, feat0_], w_in, w_out, wide)

    pair2 = jnp.stack([e2, after(a2, near, e3)])
    both1, e3 = after(both1, pair2), after(e3, pair2)
    both2, a3, both1_, pair2_ = move_b(pair2), move_a(e3), swap(both1), swap(pair2)
    cot0 = [pair0, both0, pair0_, both0_]
    cot1 = [pair1, both1, pair1_, both1_]
    hidden01, running = backward([cot0, cot1], [[feat0, feat0_], cot1], [0, wide], None, e3, pair2_)

    pair3 = jnp.stack([e3, after(a3, running)])
    both2 = after(both2, pair3)
    both3, both2_, pair3_, got = move_b(pair3), swap(both2), swap(pair3), swap(after(away, pair3))
    near = near + got.astype(F32)
    cot2 = [pair2, both2, pair2_, both2_]
    hidden2, running = backward([cot2], [cot2], [wide], running, near, pair3_)
    both3 = after(both3, running)
    both3_ = swap(both3)
    moved = move_b(after(near, running)[2:].astype(BF16))
    cot3 = [pair3, both3, pair3_, both3_]
    hidden3, running = backward([cot3], [cot3], [wide], running)

    rows = w_in.shape[0] // 4
    parts = [lax.dynamic_slice_in_dim(running, (z ^ k) * rows, rows, 0) for k in range(4)]
    sent = [parts[k].astype(BF16) for k in (1, 2, 3)]
    moved_parts = [move_z(sent[k - 1], k) for k in (1, 2, 3)]
    moved = after(moved, running, *sent).astype(F32)
    first = (near[1] + moved[1]).astype(BF16)
    last = move_a(first)
    grad_out = grad_out_of(after(blocks, first), [hidden01, hidden2, hidden3], [cot0, cot1, cot2, cot3], wide)
    last, *moved_parts = lax.optimization_barrier((last, *moved_parts, grad_out))[:4]
    grad_in = jnp.zeros((rows, 4 * units), F32)
    for k, part in enumerate(parts[:1] + moved_parts):
        grad_in = lax.dynamic_update_slice_in_dim(grad_in, part.astype(F32), (z ^ k) * units, 1)
    mixed_out = (near[0] + moved[0] + last.astype(F32)).astype(BF16)
    return (mixed_out, grad_in, grad_out)


def summed_shards(lookup_ids, bag_lengths, feature_widths, tables, w_in, w_out, cotangent):
    pooled = pool_local(lookup_ids, bag_lengths, feature_widths, tables[0])
    features = lax.all_gather(pooled, PLANE, axis=1, tiled=True)
    preact = jnp.dot(features, w_in, preferred_element_type=F32)
    hidden = jax.nn.silu(preact).astype(BF16)
    partial_out = jnp.dot(hidden, w_out, preferred_element_type=F32)
    reduced = lax.psum_scatter(partial_out, PLANE, scatter_dimension=1, tiled=True)
    mixed_out = reduced.astype(BF16)
    whole_grad = lax.all_gather(cotangent, PLANE, axis=1, tiled=True)
    grad_hidden = lax.dot_general(whole_grad, w_out, COLS_NT, preferred_element_type=F32)
    grad_preact = (grad_hidden * silu_slope(preact)).astype(BF16)
    term_in = lax.dot_general(features, grad_preact, ROWS_TN, preferred_element_type=F32)
    term_out = lax.dot_general(hidden, whole_grad, ROWS_TN, preferred_element_type=F32)
    grad_in = lax.psum_scatter(term_in, "dp", scatter_dimension=0, tiled=True)
    grad_out = lax.psum_scatter(term_out, "dp", scatter_dimension=0, tiled=True)
    return (mixed_out, grad_in, grad_out)


def solution(mesh):
    sizes = (mesh.shape["table"], mesh.shape["tensor"], mesh.shape["dp"])
    return jax.shard_map(
        spread_shards if sizes == (4, 2, 4) else summed_shards,
        mesh=mesh,
        in_specs=(
            P("dp", "table", None),
            P("dp", "table"),
            P(),
            P("table", None, "tensor"),
            P(None, PLANE),
            P(PLANE, None),
            P("dp", PLANE),
        ),
        out_specs=(
            P("dp", PLANE),
            P("dp", PLANE),
            P(("table", "tensor", "dp"), None),
        ),
        check_vma=False,
    )
```

```python
import functools

import jax
import jax.numpy as jnp
from jax import lax
from jax.experimental import pallas as pl
from jax.experimental.pallas import tpu as pltpu
from jax.sharding import PartitionSpec as P

F32 = jnp.float32
BF16 = jnp.bfloat16
PLANE = ("table", "tensor")
VMEM_MIB = 50
ROWS_TN = (((0,), (0,)), ((), ()))
COLS_NT = (((1,), (1,)), ((), ()))


def silu_slope(preact):
    sigmoid_part = jax.nn.sigmoid(preact)
    return sigmoid_part * (1.0 + preact * (1.0 - sigmoid_part))


def cost(flops, bytes_accessed, transcendentals):
    return pl.CostEstimate(flops=flops, bytes_accessed=bytes_accessed, transcendentals=transcendentals)


def params(mib):
    return pltpu.CompilerParams(vmem_limit_bytes=mib * 1024 * 1024)


def pool_kernel(key_ref, len_ref, width_ref, table_ref, out_ref, counts_ref, *, group, low):
    samples, columns = out_ref.shape
    slots = key_ref.shape[1]
    bag = slots // group
    high = table_ref.shape[0] // low
    rows = lax.broadcasted_iota(jnp.int32, (high * group, slots), 0)
    low_rows = lax.broadcasted_iota(jnp.int32, (low, slots), 0)
    lane = lax.broadcasted_iota(jnp.int32, (1, slots), 1)
    member, slot = lane // bag, lax.rem(lane, bag)
    group_rows = lax.broadcasted_iota(jnp.int32, (group, slots), 0)

    def one_group(g, carry):
        first = pl.multiple_of(g * group, group)
        lengths = jnp.where(group_rows == member, len_ref[pl.ds(first, group), :], 0)
        in_bag = slot < jnp.sum(lengths, axis=0, keepdims=True)
        key = key_ref[pl.ds(g, 1), :]
        hit_high = (rows == jnp.where(in_bag, (key // low) * group + member, -1)).astype(BF16)
        hit_low = (low_rows == lax.rem(key, low)).astype(BF16)
        counts = lax.dot_general(hit_high, hit_low, COLS_NT, preferred_element_type=F32).astype(BF16)
        for h in range(high):
            counts_ref[h, pl.ds(first, group), :] = counts[h * group : (h + 1) * group, :]
        return carry

    lax.fori_loop(0, samples // group, one_group, 0, unroll=4)
    total = jnp.zeros(out_ref.shape, F32)
    for h in range(high):
        total += jnp.dot(
            counts_ref[h], table_ref[h * low : (h + 1) * low, :], preferred_element_type=F32
        )
    pooled = total / len_ref[...].astype(F32)
    position = lax.axis_index("tensor") * columns + lax.broadcasted_iota(jnp.int32, pooled.shape, 1)
    out_ref[...] = jnp.where(position < width_ref[lax.axis_index("table")], pooled, 0.0).astype(BF16)


def pool_local(lookup_ids, bag_lengths, feature_widths, embedding):
    samples, unused, bag = lookup_ids.shape
    vocab, columns = embedding.shape
    low, group = 256, 16
    high = vocab // low
    return pl.pallas_call(
        functools.partial(pool_kernel, group=group, low=low),
        out_shape=jax.ShapeDtypeStruct((samples, columns), BF16),
        in_specs=[
            pl.BlockSpec(memory_space=pltpu.VMEM),
            pl.BlockSpec(memory_space=pltpu.VMEM),
            pl.BlockSpec(memory_space=pltpu.SMEM),
            pl.BlockSpec(memory_space=pltpu.VMEM),
        ],
        out_specs=pl.BlockSpec(memory_space=pltpu.VMEM),
        scratch_shapes=[pltpu.VMEM((high, samples, low), BF16)],
        compiler_params=params(VMEM_MIB),
        cost_estimate=cost(20 * samples * vocab * columns, 2 * vocab * columns, 0),
        name="pool",
    )(lookup_ids.reshape(samples // group, group * bag), bag_lengths, feature_widths, embedding)


def carry_kernel(block_ref, feat_ref, out_ref):
    wide = block_ref.shape[1]
    out_ref[:, :wide] = block_ref[...]
    out_ref[:, wide:] = feat_ref[...]


def carry(block, feat, weight):
    in_vmem = pl.BlockSpec(memory_space=pltpu.VMEM)
    samples, wide = block.shape
    return pl.pallas_call(
        carry_kernel,
        out_shape=jax.ShapeDtypeStruct((samples, wide + feat.shape[1]), BF16),
        in_specs=[in_vmem, in_vmem],
        out_specs=in_vmem,
        cost_estimate=cost(weight * 10**9, 0, 0),
        name="carry",
    )(block, feat)


def block_copies(place_ref, refs, first, width, buffer, sem, in_place):
    copies = []
    each = 8 // len(refs)
    for j in range(8):
        to = pl.multiple_of(place_ref[j] * width, width) if in_place else j * width
        source = refs[j // each].at[j % each, :, pl.ds(first, width)]
        copies.append(pltpu.make_async_copy(source, buffer.at[:, pl.ds(to, width)], sem.at[j]))
    return copies


def start_all(copies):
    for c in copies:
        c.start()


def wait_all(copies):
    for c in copies:
        c.wait()


def forward_kernel(
    place_ref, feat_ref, other_feat_ref, w_in_ref, w_out_ref, away_ref, near_ref,
    feat_buf, w_in_buf, hidden_buf, w_out_buf, away_buf, near_buf,
    feat_sem, w_in_sem, w_out_sem, away_sem, near_sem,
):
    pieces, samples, step = w_in_buf.shape[0], hidden_buf.shape[0], w_in_buf.shape[2]
    buffers, wide = w_out_buf.shape[0], w_out_buf.shape[2]
    half = away_ref.shape[0]
    feat_copies = block_copies(
        place_ref, [feat_ref, other_feat_ref], 0, feat_ref.shape[2], feat_buf, feat_sem, True
    )
    w_in_copies = [
        pltpu.make_async_copy(w_in_ref.at[:, pl.ds(i * step, step)], w_in_buf.at[i], w_in_sem.at[i])
        for i in range(pieces)
    ]
    slots = [*range(half, 2 * half), *range(half)]
    w_out_copies = []
    for i, slot in enumerate(slots):
        column = pl.ds(pl.multiple_of(place_ref[slot] * wide, wide), wide)
        w_out_copies.append(
            pltpu.make_async_copy(w_out_ref.at[:, column], w_out_buf.at[i % buffers], w_out_sem.at[i % buffers])
        )
    start_all(feat_copies + w_in_copies + w_out_copies[: buffers - 1])
    wait_all(feat_copies)
    for i in range(pieces):
        w_in_copies[i].wait()
        preact = jnp.dot(feat_buf[...], w_in_buf[i], preferred_element_type=F32)
        hidden_buf[:, i * step : (i + 1) * step] = jax.nn.silu(preact).astype(BF16)
    out_copies = []
    for i in range(2 * half):
        if i + buffers - 1 < 2 * half:
            w_out_copies[i + buffers - 1].start()
        w_out_copies[i].wait()
        product = jnp.dot(hidden_buf[...], w_out_buf[i % buffers], preferred_element_type=F32)
        if i < half:
            away_buf[i] = product.astype(BF16)
            out_copies.append(pltpu.make_async_copy(away_buf.at[i], away_ref.at[i], away_sem.at[i]))
        else:
            near_buf[i - half] = product
            out_copies.append(pltpu.make_async_copy(near_buf.at[i - half], near_ref.at[i - half], near_sem.at[i - half]))
        out_copies[-1].start()
    wait_all(out_copies)


def forward(place, feat_blocks, w_in, w_out, wide):
    samples = feat_blocks[0].shape[1]
    depth, units = w_in.shape
    step, buffers = units // 4, 3
    any_space = pl.BlockSpec(memory_space=pl.ANY)
    return pl.pallas_call(
        forward_kernel,
        out_shape=(
            jax.ShapeDtypeStruct((4, samples, wide), BF16),
            jax.ShapeDtypeStruct((4, samples, wide), F32),
        ),
        in_specs=[pl.BlockSpec(memory_space=pltpu.SMEM)] + [any_space] * 4,
        out_specs=(any_space, any_space),
        scratch_shapes=[
            pltpu.VMEM((samples, depth), BF16),
            pltpu.VMEM((4, depth, step), BF16),
            pltpu.VMEM((samples, units), BF16),
            pltpu.VMEM((buffers, units, wide), BF16),
            pltpu.VMEM((4, samples, wide), BF16),
            pltpu.VMEM((4, samples, wide), F32),
            pltpu.SemaphoreType.DMA((8,)),
            pltpu.SemaphoreType.DMA((4,)),
            pltpu.SemaphoreType.DMA((buffers,)),
            pltpu.SemaphoreType.DMA((4,)),
            pltpu.SemaphoreType.DMA((4,)),
        ],
        compiler_params=params(VMEM_MIB),
        cost_estimate=cost(
            2 * samples * units * (depth + 8 * wide), 2 * units * (depth + 8 * wide), samples * units
        ),
        name="forward",
    )(place, *feat_blocks, w_in, w_out)


def chunk_kernel(place_ref, *refs, wide, firsts, feat_counts, add, split):
    chunks = len(firsts)
    cot_refs, refs = [refs[4 * k : 4 * k + 4] for k in range(chunks)], refs[4 * chunks :]
    feat_refs = []
    for n in feat_counts:
        feat_refs.append(refs[:n])
        refs = refs[n:]
    w_out_ref, w_in_ref, refs = refs[0], refs[1], refs[2:]
    sum_ref, refs = (refs[0], refs[1:]) if add else (None, refs)
    hidden_ref, refs = refs[0], refs[1:]
    (sent_ref, kept_ref), refs = (refs[:2], refs[2:]) if split else ((None, None), refs)
    grad_in_ref, cot_buf, w_out_buf, feat_buf, w_in_buf, sum_buf, cot_sem, w_sem, feat_sem, sem = refs
    units = hidden_ref.shape[0]
    samples = cot_buf.shape[0] // chunks
    row = pl.ds(pl.multiple_of(place_ref[8] * units, units), units)
    cot_copies, feat_copies, w_copies = [], [], []
    for k in range(chunks):
        rows = pl.ds(k * samples, samples)
        cot_copies.append(block_copies(place_ref, cot_refs[k], 0, wide, cot_buf.at[rows], cot_sem.at[k], False))
        feat_copies += block_copies(
            place_ref, feat_refs[k], firsts[k], feat_buf.shape[1] // 8, feat_buf.at[rows], feat_sem.at[k], True
        )
    for j in range(8):
        column = pl.ds(pl.multiple_of(place_ref[j] * wide, wide), wide)
        w_copies.append(
            pltpu.make_async_copy(w_out_ref.at[row, column], w_out_buf.at[:, pl.ds(j * wide, wide)], w_sem.at[j])
        )
    w_in_copy = pltpu.make_async_copy(w_in_ref.at[:, row], w_in_buf, sem.at[0])
    start_all(feat_copies)
    w_in_copy.start()
    early = [c for copies in cot_copies for c in copies[:4]] + w_copies[:4]
    late = [c for copies in cot_copies for c in copies[4:]] + w_copies[4:]
    start_all(early + late)
    if add:
        sum_copy = pltpu.make_async_copy(sum_ref, sum_buf, sem.at[1])
        sum_copy.start()

    wait_all(feat_copies)
    w_in_copy.wait()
    preact = jnp.dot(feat_buf[...], w_in_buf[...], preferred_element_type=F32)
    hidden_ref[...] = jax.nn.silu(preact).astype(BF16).T
    slope = silu_slope(preact)
    middle = 4 * wide
    wait_all(early)
    grad_hidden = lax.dot_general(
        cot_buf[:, :middle], w_out_buf[:, :middle], COLS_NT, preferred_element_type=F32
    )
    wait_all(late)
    grad_hidden += lax.dot_general(
        cot_buf[:, middle:], w_out_buf[:, middle:], COLS_NT, preferred_element_type=F32
    )
    grad_preact = (grad_hidden * slope).astype(BF16)
    term = lax.dot_general(feat_buf[...], grad_preact, ROWS_TN, preferred_element_type=F32)
    if add:
        sum_copy.wait()
        term += sum_buf[...]
    grad_in_ref[...] = term
    if split:
        rows = kept_ref.shape[0]
        for k in range(split):
            other = lax.bitwise_xor(place_ref[8], k)
            block = grad_in_ref[pl.ds(pl.multiple_of(other * rows, rows), rows), :]
            if k == 0:
                kept_ref[...] = block
            else:
                sent_ref[k - 1] = block.astype(BF16)


def chunk_backward(place, cot, feat, firsts, w_out, w_in, running, units, wide, split):
    chunks = len(cot)
    samples = chunks * cot[0][0].shape[1]
    depth = w_in.shape[0]
    add = running is not None
    feat_counts = [len(f) for f in feat]
    operands = [v for c in cot for v in c] + [v for f in feat for v in f] + [w_out, w_in]
    operands += [running] if add else []
    sums, held = [jax.ShapeDtypeStruct((depth, units), F32)], []
    if split:
        rows = depth // split
        sums = [jax.ShapeDtypeStruct((split - 1, rows, units), BF16), jax.ShapeDtypeStruct((rows, units), F32)]
        held = [pltpu.VMEM((depth, units), F32)]
    in_vmem = pl.BlockSpec(memory_space=pltpu.VMEM)
    return pl.pallas_call(
        functools.partial(chunk_kernel, wide=wide, firsts=firsts, feat_counts=feat_counts, add=add, split=split),
        out_shape=(jax.ShapeDtypeStruct((units, samples), BF16), *sums),
        in_specs=[pl.BlockSpec(memory_space=pltpu.SMEM)] + [pl.BlockSpec(memory_space=pl.ANY)] * len(operands),
        out_specs=(in_vmem,) * (1 + len(sums)),
        scratch_shapes=held + [
            pltpu.VMEM((samples, 8 * wide), BF16),
            pltpu.VMEM((units, 8 * wide), BF16),
            pltpu.VMEM((samples, depth), BF16),
            pltpu.VMEM((depth, units), BF16),
            pltpu.VMEM((depth, units) if add else (8, 128), F32),
            pltpu.SemaphoreType.DMA((chunks, 8)),
            pltpu.SemaphoreType.DMA((8,)),
            pltpu.SemaphoreType.DMA((chunks, 8)),
            pltpu.SemaphoreType.DMA((2,)),
        ],
        compiler_params=params(VMEM_MIB),
        cost_estimate=cost(
            2 * samples * units * (8 * wide + 2 * depth),
            2 * (samples + units) * (8 * wide + depth) + 8 * depth * units,
            2 * samples * units,
        ),
        name="chunk_backward",
    )(place, *operands)


def grad_out_kernel(place_ref, *refs, chunks):
    blocks, hidden = refs[: 4 * chunks], refs[4 * chunks : -5]
    out_ref, hidden_buf, cot_buf, hidden_sem, cot_sem = refs[-5:]
    samples, wide = cot_buf.shape[1] // chunks, out_ref.shape[1]
    j = pl.program_id(0)
    rows = [slice(k * samples, (k + 1) * samples) for k in range(chunks)]

    def fetch(slot, action):
        buffer = lax.rem(slot, 2)
        for i in range(4):

            @pl.when(slot // 2 == i)
            def _():
                for k in range(chunks):
                    source = blocks[4 * k + i].at[lax.rem(slot, 2), :, pl.ds(0, wide)]
                    action(pltpu.make_async_copy(source, cot_buf.at[buffer, rows[k]], cot_sem.at[buffer, k]))

    hidden_copies, first = [], 0
    for k, ref in enumerate(hidden):
        to = hidden_buf.at[:, pl.ds(first, ref.shape[1])]
        hidden_copies.append(pltpu.make_async_copy(ref, to, hidden_sem.at[k]))
        first += ref.shape[1]

    @pl.when(j == 0)
    def _():
        start_all(hidden_copies)
        fetch(j, lambda c: c.start())

    @pl.when(j + 1 < pl.num_programs(0))
    def _():
        fetch(j + 1, lambda c: c.start())

    @pl.when(j == 0)
    def _():
        wait_all(hidden_copies)

    fetch(j, lambda c: c.wait())
    out_ref[...] = jnp.dot(hidden_buf[...], cot_buf[lax.rem(j, 2)], preferred_element_type=F32)


def grad_out_of(place, hidden, cot_blocks, wide):
    chunks = len(cot_blocks)
    units, samples = hidden[0].shape[0], cot_blocks[0][0].shape[1]
    flat = [array for blocks in cot_blocks for array in blocks]
    return pl.pallas_call(
        functools.partial(grad_out_kernel, chunks=chunks),
        out_shape=jax.ShapeDtypeStruct((units, 8 * wide), F32),
        grid_spec=pltpu.PrefetchScalarGridSpec(
            num_scalar_prefetch=1,
            grid=(8,),
            in_specs=[pl.BlockSpec(memory_space=pl.ANY)] * (4 * chunks + len(hidden)),
            out_specs=pl.BlockSpec((units, wide), lambda j, p: (0, p[j])),
            scratch_shapes=[
                pltpu.VMEM((units, chunks * samples), BF16),
                pltpu.VMEM((2, chunks * samples, wide), BF16),
                pltpu.SemaphoreType.DMA((chunks,)),
                pltpu.SemaphoreType.DMA((2, chunks)),
            ],
        ),
        compiler_params=params(VMEM_MIB),
        cost_estimate=cost(
            2 * units * chunks * samples * 8 * wide,
            2 * chunks * samples * (8 * wide + units) + 4 * units * 8 * wide,
            0,
        ),
        name="grad_out",
    )(place, *flat, *hidden)


def plane_perms():
    first, second = [], []
    for t in range(4):
        for y in range(2):
            along_x, along_y = (t ^ 2) * 2 + y, t * 2 + (y ^ 1)
            first.append((t * 2 + y, along_x if t % 2 == 0 else along_y))
            second.append((t * 2 + y, along_y if t % 2 == 0 else along_x))
    return first, second


PERM_A, PERM_B = plane_perms()


def move_a(v):
    return lax.ppermute(v, PLANE, PERM_A)


def move_b(v):
    return lax.ppermute(v, PLANE, PERM_B)


def move_both(v):
    return lax.ppermute(v, PLANE, [(t * 2 + y, (t ^ 2) * 2 + (y ^ 1)) for t in range(4) for y in range(2)])


def swap(v):
    return lax.ppermute(v, "table", [(t, t ^ 1) for t in range(4)])


def move_z(v, k):
    return lax.ppermute(v, "dp", [(z, z ^ k) for z in range(4)])


def plane_blocks():
    t, y = lax.axis_index("table"), lax.axis_index("tensor")
    x, core = t // 2, t % 2
    blocks = []
    for dc in range(2):
        c = core ^ dc
        a_x, a_y = jnp.where(c == 0, 1, 0), jnp.where(c == 0, 0, 1)
        for dx, dy in ((0, 0), (a_x, a_y), (a_y, a_x), (1, 1)):
            blocks.append(((x ^ dx) * 2 + c) * 2 + (y ^ dy))
    return jnp.stack(blocks).astype(jnp.int32)


def after(v, *earlier):
    return lax.optimization_barrier((v,) + earlier)[0]


def spread_shards(lookup_ids, bag_lengths, feature_widths, tables, w_in, w_out, cotangent):
    z = lax.axis_index("dp")
    wide = cotangent.shape[1]
    units = w_in.shape[1] // 4
    blocks = plane_blocks()
    place = jnp.concatenate([blocks, z[None].astype(jnp.int32)])

    def backward(cot, feat, firsts, running, *earlier, split=0):
        return chunk_backward(after(place, *earlier), cot, feat, firsts, w_out, w_in, running, units, wide, split)

    s0 = cotangent
    a0, s2 = move_a(s0), move_z(s0, 2)
    pooled = pool_local(lookup_ids, bag_lengths, feature_widths, tables[0])
    pair0 = jnp.stack([s0, after(a0, pooled)])
    both0, pair1 = move_b(pair0), move_z(pair0, 1)
    pa, pooled2 = move_a(pooled), move_z(pooled, 2)
    pa, pooled2, s2 = lax.optimization_barrier((pa, pooled2, s2))

    feat_pair = jnp.stack([pooled, pa])
    e2 = carry(s2, pooled2, 5)
    feat_pair, e2 = lax.optimization_barrier((feat_pair, e2))
    a2, feat_both, e3 = move_a(e2), move_b(feat_pair), move_z(e2, 1)
    feat0 = jnp.concatenate([feat_pair, feat_both])
    feat0_, both0_ = swap(feat0), swap(after(both0, feat0))
    pair2 = jnp.stack([e2, after(a2, feat0, pair1)])
    both2, feat1 = move_b(pair2), move_z(after(feat0, pair2), 1)
    pair0_ = swap(after(pair0, pair2))
    away, near = forward(after(place, pair2, both0_, pair0_), [feat0, feat0_], w_in, w_out, wide)

    e3, both2 = lax.optimization_barrier((e3, after(both2, near)))
    a3, both2_, pair2_ = move_a(e3), swap(both2), swap(after(pair2, e3))
    both1 = move_b(after(pair1, e3))
    cot0 = [pair0, both0, pair0_, both0_]
    cot2 = [pair2, both2, pair2_, both2_]
    hidden02, running = backward([cot0, cot2], [[feat0, feat0_], cot2], [0, wide], None, e3)

    pair3 = jnp.stack([e3, after(a3, running, both1, feat1)])
    both3 = move_b(pair3)
    both1 = after(both1, pair3)
    feat1_, both1_, pair1_, got = swap(after(feat1, pair3)), swap(both1), swap(after(pair1, pair3)), swap(after(away, pair3))
    sums = [near[k] + got[k].astype(F32) for k in range(4)]
    leaving = [sums[k].astype(BF16) for k in (1, 2, 3)]
    cot1 = [pair1, both1, pair1_, both1_]
    hidden1, running = backward([cot1], [[feat1, feat1_]], [0], running, *leaving)
    both3 = after(both3, running)
    both3_, pair3_ = swap(both3), swap(after(pair3, running))
    arrived = [move_a(leaving[0]), move_b(leaving[1]), move_both(leaving[2])]
    cot3 = [pair3, both3, pair3_, both3_]
    hidden3, sent, kept = backward([cot3], [cot3], [wide], running, both3_, split=4)

    moved_parts = [move_z(sent[k - 1], k) for k in (3, 2, 1)]
    grad_out = grad_out_of(after(blocks, sent), [hidden02, hidden1, hidden3], [cot0, cot2, cot1, cot3], wide)
    late = lax.optimization_barrier((*arrived, *moved_parts, grad_out))
    grad_in = jnp.zeros((kept.shape[0], 4 * units), F32)
    for k, part in enumerate((kept,) + late[3:6][::-1]):
        grad_in = lax.dynamic_update_slice_in_dim(grad_in, part.astype(F32), (z ^ k) * units, 1)
    mixed_out = (sums[0] + late[0].astype(F32) + late[1].astype(F32) + late[2].astype(F32)).astype(BF16)
    return (mixed_out, grad_in, grad_out)


def summed_shards(lookup_ids, bag_lengths, feature_widths, tables, w_in, w_out, cotangent):
    pooled = pool_local(lookup_ids, bag_lengths, feature_widths, tables[0])
    features = lax.all_gather(pooled, PLANE, axis=1, tiled=True)
    preact = jnp.dot(features, w_in, preferred_element_type=F32)
    hidden = jax.nn.silu(preact).astype(BF16)
    partial_out = jnp.dot(hidden, w_out, preferred_element_type=F32)
    reduced = lax.psum_scatter(partial_out, PLANE, scatter_dimension=1, tiled=True)
    mixed_out = reduced.astype(BF16)
    whole_grad = lax.all_gather(cotangent, PLANE, axis=1, tiled=True)
    grad_hidden = lax.dot_general(whole_grad, w_out, COLS_NT, preferred_element_type=F32)
    grad_preact = (grad_hidden * silu_slope(preact)).astype(BF16)
    term_in = lax.dot_general(features, grad_preact, ROWS_TN, preferred_element_type=F32)
    term_out = lax.dot_general(hidden, whole_grad, ROWS_TN, preferred_element_type=F32)
    grad_in = lax.psum_scatter(term_in, "dp", scatter_dimension=0, tiled=True)
    grad_out = lax.psum_scatter(term_out, "dp", scatter_dimension=0, tiled=True)
    return (mixed_out, grad_in, grad_out)


def solution(mesh):
    sizes = (mesh.shape["table"], mesh.shape["tensor"], mesh.shape["dp"])
    return jax.shard_map(
        spread_shards if sizes == (4, 2, 4) else summed_shards,
        mesh=mesh,
        in_specs=(
            P("dp", "table", None),
            P("dp", "table"),
            P(),
            P("table", None, "tensor"),
            P(None, PLANE),
            P(PLANE, None),
            P("dp", PLANE),
        ),
        out_specs=(
            P("dp", PLANE),
            P("dp", PLANE),
            P(("table", "tensor", "dp"), None),
        ),
        check_vma=False,
    )
```
